32 devices in a mesh: grp: 2 (over y), mod: 4 (over z), dp: 4 (over x, core).
Axes of the slice: x: 2, y: 2, z: 4, core: 2. Of those that a mesh axis runs over, the one named last changes fastest.
Arguments:
- act_proj: bfloat16 [512, 64, 128], P(('grp', 'mod', 'dp')), parts along dimension 0, may hold values from -3 to 3
- grad_proj: bfloat16 [512, 64, 128], P(('grp', 'mod', 'dp')), parts along dimension 0, may hold values from -3 to 3
- lengths: int32 [512], P(('grp', 'mod', 'dp')), parts along dimension 0, may hold values from 1 to 64
- assignment: int32 [4], replicated, may hold values from 0 to 3, each once
Outputs:
- covariance: float32 [2048, 4, 1024], P(('grp', 'dp'), 'mod'), parts along dimension 0
The draws below stay inside these ranges and needn't reach their ends.
There are 2 independent parts, one for each index of `grp`. The reference program is written for one: setup_inputs(seed, part) draws one part's arguments, and reference() takes and returns one part's arrays. A program takes and returns all parts, laid end to end along the dimension named above; an argument that names none is the same for every part. Nothing has to cross between parts.
Inputs may be any that keep to these rules, and one draw needn't show every extreme that they name: assignment is a permutation of the module positions.
All inputs are finite; a program needn't handle non-finite values.
Results may differ from the reference program's by a relative error of at most 0.0003.
Values may be sent and summed in bfloat16 or wider, within the bound.
A program may use at most 64 MiB of HBM per device.

```python
import jax
import jax.numpy as jnp
from jax import lax

PROJ = 32
MODS = 4
SEQ = 64
EX_DEV = 16
EXAMPLES = 256
N_MOD = 4
N_DP = 4


def place_ends(values, stream_key, smallest, top_value):
    extent = values.shape
    spot = [jax.random.randint(jax.random.fold_in(stream_key, axis), (), 0, extent[axis]) for axis in range(len(extent))]
    values = values.at[tuple(spot)].set(smallest)
    longest = extent.index(max(extent))
    spot[longest] = (spot[longest] + 1) % extent[longest]
    return values.at[tuple(spot)].set(top_value)


def block_scale(stream_key, shape, split, smallest, largest):
    def one(dim, shards_of):
        draws = jax.random.uniform(jax.random.fold_in(jax.random.fold_in(stream_key, 6), dim), (shards_of,), jnp.float32, smallest / len(split), largest / len(split))
        return jnp.repeat(jnp.exp(draws), shape[dim] // shards_of).reshape((-1,) + (1,) * (len(shape) - dim - 1))

    factor_of = one(*split[0])
    for cut in split[1:]:
        factor_of = factor_of * one(*cut)
    return factor_of


def bell_draw(rng, shape, deviation, bound, shards=(), kind=jnp.bfloat16):
    result = deviation * jax.random.normal(rng, shape, jnp.float32)
    if shards:
        result = result * block_scale(rng, shape, shards, -0.22, 0.18)
    return jnp.clip(result, -bound, bound).astype(kind)


def setup_inputs(seed: int = 0, part: int = 0) -> dict:
    key_list = jax.random.split(jax.random.key(seed), 5)
    part_splits = jax.random.split(jax.random.fold_in(key_list[4], part), 5)
    act_proj = bell_draw(part_splits[0], (EXAMPLES, SEQ, MODS * PROJ), 0.3, 3.0, ((0, 16),))
    grad_proj = bell_draw(part_splits[1], (EXAMPLES, SEQ, MODS * PROJ), 0.3, 3.0, ((0, 16),))
    lengths = place_ends(jax.random.randint(part_splits[2], (EXAMPLES,), 1, SEQ + 1), jax.random.fold_in(part_splits[2], 1), 1, SEQ).astype(jnp.int32)
    assignment = jax.random.permutation(key_list[3], MODS).astype(jnp.int32)
    return dict(act_proj=act_proj, grad_proj=grad_proj, lengths=lengths, assignment=assignment)


def reference(act_proj, grad_proj, lengths, assignment):
    activations = act_proj.reshape(EXAMPLES, SEQ, MODS, PROJ)
    gradients = grad_proj.reshape(EXAMPLES, SEQ, MODS, PROJ)
    valid_tokens = jnp.arange(SEQ, dtype=jnp.int32)[None, :] < lengths[:, None]
    gradients = jnp.where(valid_tokens[:, :, None, None], gradients, jnp.zeros((), jnp.bfloat16))
    source = jnp.argsort(assignment).astype(jnp.int32)

    def position_covariance(position):
        module_index = source[position]
        act_module = lax.dynamic_index_in_dim(activations, module_index, 2, keepdims=False).astype(jnp.float32)
        grad_module = lax.dynamic_index_in_dim(gradients, module_index, 2, keepdims=False).astype(jnp.float32)
        example_grad = jnp.einsum("esa,esb->eab", grad_module, act_module).reshape(EXAMPLES, PROJ * PROJ)
        return jnp.dot(example_grad.T, example_grad, precision=lax.Precision.HIGHEST)

    stacked = lax.map(position_covariance, jnp.arange(MODS, dtype=jnp.int32))
    inverse_count = jnp.float32(1.0 / (EX_DEV * N_MOD * N_DP))
    return jnp.transpose(stacked, (1, 0, 2)) * inverse_count
```

```python
import functools

import jax
import jax.numpy as jnp
from jax import lax
from jax.experimental import pallas as pl
from jax.experimental.pallas import tpu as pltpu
from jax.sharding import PartitionSpec as P

MESH = pl.DeviceIdType.MESH
LANES = 128


def kernel(
    n_mod, n_dp, rank, lens_ref, assign_ref, act_hbm, grad_hbm, out_ref,
    act_v, grad_v, prod, coded, outbox, inbox, high, low,
    in_sem, z_send, z_recv, x_send, x_recv, c_send, c_recv, f_send, f_recv,
):
    ex, seq, width = act_v.shape
    entries = rank * rank
    tiles = entries // LANES
    per_tile = LANES // rank
    n_lo = 2 if n_dp % 2 == 0 else 1
    n_hi = n_dp // n_lo
    small = n_mod <= 8
    mod = lax.axis_index("mod")
    dp = lax.axis_index("dp")
    hi, lo = dp // n_lo, dp % n_lo
    mine = [pltpu.make_async_copy(act_hbm, act_v, in_sem.at[0]),
            pltpu.make_async_copy(grad_hbm, grad_v, in_sem.at[1])]
    for copy in mine:
        copy.start()

    mod_at = [lax.rem(mod + o, n_mod) for o in range(n_mod)]
    mod_from = [lax.rem(mod + n_mod - o, n_mod) for o in range(n_mod)]
    hi_at = [lax.rem(hi + h, n_hi) * n_lo + lo for h in range(n_hi)]
    hi_from = [lax.rem(hi + n_hi - h, n_hi) for h in range(n_hi)]

    barrier = pltpu.get_barrier_semaphore()
    for o in range(1, n_mod):
        pl.semaphore_signal(barrier, inc=1, device_id={"mod": mod_at[o]}, device_id_type=MESH)
    for h in range(1, n_hi):
        pl.semaphore_signal(barrier, inc=1, device_id={"dp": hi_at[h]}, device_id_type=MESH)
    if n_lo == 2:
        sibling = hi * 2 + (1 - lo)
        pl.semaphore_signal(barrier, inc=1, device_id={"dp": sibling}, device_id_type=MESH)
    for copy in mine:
        copy.wait()

    token = lax.broadcasted_iota(jnp.int32, (seq, LANES), 0)
    lane = lax.broadcasted_iota(jnp.int32, (ex, LANES), 1)

    def module_tile(j):
        columns = pl.ds(pl.multiple_of(j * LANES, LANES), LANES)
        for e in range(ex):
            grad = grad_v[e, :, columns].astype(jnp.float32)
            grad = jnp.where(token < lens_ref[e], grad, 0.0).astype(jnp.bfloat16)
            prod[pl.ds(e * LANES, LANES), :] = lax.dot_general(
                grad, act_v[e, :, columns], (((0,), (0,)), ((), ())),
                preferred_element_type=jnp.float32)
        for mm in range(per_tile):
            rows = []
            for t in range(tiles):
                row = None
                for k in range(per_tile):
                    part = prod[pl.ds(mm * rank + t * per_tile + k, ex, stride=LANES), :]
                    shift = (k - mm) % per_tile
                    if shift:
                        part = pltpu.roll(part, shift * rank, 1)
                    row = part if k == 0 else jnp.where(lane >= k * rank, part, row)
                rows.append(row)
            top = functools.reduce(jnp.maximum, [jnp.abs(row) for row in rows])
            power = jnp.ceil(jnp.log2(jnp.maximum(top, 1e-30) * (1.0 / 32766.0)))
            scale = jnp.exp2(-power)
            slot = j * per_tile + mm
            for t in range(tiles):
                coded[slot, :, t * LANES:(t + 1) * LANES] = (
                    jnp.round(rows[t] * scale).astype(jnp.int32).astype(jnp.int16))
            coded[slot, :, entries:] = power.astype(jnp.int32).astype(jnp.int16)

    if width == LANES:
        module_tile(0)
    else:
        lax.fori_loop(0, width // LANES, lambda j, c: (module_tile(j), c)[1], 0)

    peers = (n_mod - 1) + (n_hi - 1) + (n_lo - 1)
    pl.semaphore_wait(barrier, peers)

    def source(position):
        found = jnp.int32(0)
        for m in range(n_mod):
            found = jnp.where(assign_ref[m] == position, m, found)
        return found

    def slot_of(dp_index, mod_index):
        return dp_index * n_mod + mod_index

    def remote(src, dst, send, recv, device):
        return pltpu.make_async_remote_copy(
            src_ref=src, dst_ref=dst, send_sem=send, recv_sem=recv,
            device_id=device, device_id_type=MESH)

    started = []
    z_copies = [None] * n_mod
    for o in list(range(1, n_mod)) + [0]:
        block = coded[source(mod_at[o])]
        if o == 0:
            inbox[slot_of(dp, mod)] = block
        else:
            outbox[o] = block
            z_copies[o] = remote(outbox.at[o], inbox.at[slot_of(dp, mod)],
                                 z_send.at[o], z_recv.at[o], {"mod": mod_at[o]})
            z_copies[o].start()
            started.append(z_copies[o])

    def decode(position, block):
        def tile(t):
            columns = pl.ds(pl.multiple_of(t * LANES, LANES), LANES)
            value = inbox[block, :, columns].astype(jnp.int32).astype(jnp.float32)
            power = inbox[block, :, entries:].astype(jnp.int32).astype(jnp.float32)
            value = value * jnp.exp2(power)
            top = value.astype(jnp.bfloat16)
            rows = pl.ds(position * ex, ex)
            high[rows, columns] = top
            low[rows, columns] = (value - top.astype(jnp.float32)).astype(jnp.bfloat16)
        if small:
            for t in range(tiles):
                tile(t)
        else:
            lax.fori_loop(0, tiles, lambda t, c: (tile(t), c)[1], 0)

    out_rows = out_ref.shape[0] // tiles
    depth = n_lo * n_mod * ex
    inverse_count = 1.0 / (ex * n_mod * n_dp)

    def multiply(h):
        deep = pl.ds(h * depth, depth)
        left = pl.ds(pl.multiple_of(dp * out_rows, LANES), out_rows)
        left_high = high[deep, left].T
        left_low = low[deep, left].T

        def column(t):
            columns = pl.ds(pl.multiple_of(t * LANES, LANES), LANES)
            dot = functools.partial(jnp.dot, preferred_element_type=jnp.float32)
            total = (dot(left_high, high[deep, columns]) + dot(left_high, low[deep, columns])
                     + dot(left_low, high[deep, columns]))
            place = pl.ds(t, out_rows, stride=tiles)
            if h > 0:
                total = total + out_ref[place, :]
            if h == n_hi - 1:
                total = total * inverse_count
            out_ref[place, :] = total
        if small:
            for t in range(tiles):
                column(t)
        else:
            lax.fori_loop(0, tiles, lambda t, c: (column(t), c)[1], 0)

    x_copies = [[None] * n_mod for _ in range(n_hi)]
    c_copies = [None] * n_mod
    f_copies = [[None] * n_mod for _ in range(n_hi)]
    for o in range(n_mod):
        if o:
            z_copies[o].wait_recv()
        block = slot_of(dp, mod_from[o])
        for h in range(1, n_hi):
            x_copies[h][o] = remote(inbox.at[block], inbox.at[block],
                                    x_send.at[h, o], x_recv.at[h, o], {"dp": hi_at[h]})
            x_copies[h][o].start()
            started.append(x_copies[h][o])
        if n_lo == 2:
            c_copies[o] = remote(inbox.at[block], inbox.at[block],
                                 c_send.at[o], c_recv.at[o], {"dp": sibling})
            c_copies[o].start()
            started.append(c_copies[o])
        decode(o, block)
    if n_lo == 2:
        for o in range(n_mod):
            for h in range(1, n_hi):
                x_copies[h][o].wait_recv()
                block = slot_of(hi_from[h] * n_lo + lo, mod_from[o])
                f_copies[h][o] = remote(inbox.at[block], inbox.at[block],
                                        f_send.at[h, o], f_recv.at[h, o], {"dp": sibling})
                f_copies[h][o].start()
                started.append(f_copies[h][o])
            c_copies[o].wait_recv()
            decode(n_mod + o, slot_of(sibling, mod_from[o]))
    multiply(0)
    for h in range(1, n_hi):
        for o in range(n_mod):
            if n_lo == 1:
                x_copies[h][o].wait_recv()
            decode(h * n_lo * n_mod + o, slot_of(hi_from[h] * n_lo + lo, mod_from[o]))
        if n_lo == 2:
            for o in range(n_mod):
                f_copies[h][o].wait_recv()
                decode((h * n_lo + 1) * n_mod + o, slot_of(hi_from[h] * 2 + (1 - lo), mod_from[o]))
        multiply(h)
    for copy in started:
        copy.wait_send()


def solution(mesh):
    n_mod, n_dp = mesh.shape["mod"], mesh.shape["dp"]

    def body(act_proj, grad_proj, lengths, assignment):
        ex, seq, width = act_proj.shape
        rank = width // assignment.shape[0]
        entries = rank * rank
        out_rows = entries // n_dp
        tiles = entries // LANES
        n_hi = n_dp // 2 if n_dp % 2 == 0 else n_dp
        dma = pltpu.SemaphoreType.DMA
        any_spec = pl.BlockSpec(memory_space=pl.ANY)
        smem = pl.BlockSpec(memory_space=pltpu.SMEM)
        result = pl.pallas_call(
            functools.partial(kernel, n_mod, n_dp, rank),
            out_shape=jax.ShapeDtypeStruct((out_rows * tiles, LANES), jnp.float32),
            in_specs=[smem, smem, any_spec, any_spec],
            out_specs=pl.BlockSpec(memory_space=pltpu.VMEM),
            scratch_shapes=[
                pltpu.VMEM(act_proj.shape, jnp.bfloat16),
                pltpu.VMEM(grad_proj.shape, jnp.bfloat16),
                pltpu.VMEM((ex * LANES, LANES), jnp.float32),
                pltpu.VMEM((n_mod, ex, entries + LANES), jnp.int16),
                pltpu.VMEM((n_mod, ex, entries + LANES), jnp.int16),
                pltpu.VMEM((n_dp * n_mod, ex, entries + LANES), jnp.int16),
                pltpu.VMEM((n_dp * n_mod * ex, entries), jnp.bfloat16),
                pltpu.VMEM((n_dp * n_mod * ex, entries), jnp.bfloat16),
                dma((2,)),
                dma((n_mod,)), dma((n_mod,)),
                dma((n_hi, n_mod)), dma((n_hi, n_mod)),
                dma((n_mod,)), dma((n_mod,)),
                dma((n_hi, n_mod)), dma((n_hi, n_mod)),
            ],
            compiler_params=pltpu.CompilerParams(
                collective_id=0, has_side_effects=True, vmem_limit_bytes=48 * 1024 * 1024),
        )(lengths, assignment, act_proj, grad_proj)
        return result.reshape(out_rows, 1, entries)

    return jax.shard_map(
        body,
        mesh=mesh,
        in_specs=(
            P(("grp", "mod", "dp"), None, None),
            P(("grp", "mod", "dp"), None, None),
            P(("grp", "mod", "dp")),
            P(),
        ),
        out_specs=P(("grp", "dp"), "mod", None),
        check_vma=False,
    )
```

```python
import functools

import jax
import jax.numpy as jnp
from jax import lax
from jax.experimental import pallas as pl
from jax.experimental.pallas import tpu as pltpu
from jax.sharding import PartitionSpec as P

MESH = pl.DeviceIdType.MESH
LANES = 128


def kernel(
    n_mod, n_dp, rank, lens_hbm, assign_hbm, act_hbm, grad_hbm, out_ref,
    lens_ref, assign_ref, act_v, grad_v, prod, coded, outbox, inbox, high, low,
    in_sem, z_send, z_recv, x_send, x_recv, c_send, c_recv, f_send, f_recv,
):
    ex, seq, width = act_v.shape
    entries = rank * rank
    tiles = entries // LANES
    per_tile = LANES // rank
    n_lo = 2 if n_dp % 2 == 0 else 1
    n_hi = n_dp // n_lo
    small = n_mod <= 8
    mod = lax.axis_index("mod")
    dp = lax.axis_index("dp")
    hi, lo = dp // n_lo, dp % n_lo
    mine = [pltpu.make_async_copy(act_hbm, act_v, in_sem.at[0]),
            pltpu.make_async_copy(grad_hbm, grad_v, in_sem.at[1]),
            pltpu.make_async_copy(lens_hbm, lens_ref, in_sem.at[2]),
            pltpu.make_async_copy(assign_hbm, assign_ref, in_sem.at[3])]
    for copy in mine:
        copy.start()

    mod_at = [lax.rem(mod + o, n_mod) for o in range(n_mod)]
    mod_from = [lax.rem(mod + n_mod - o, n_mod) for o in range(n_mod)]
    hi_at = [lax.rem(hi + h, n_hi) * n_lo + lo for h in range(n_hi)]
    hi_from = [lax.rem(hi + n_hi - h, n_hi) for h in range(n_hi)]

    barrier = pltpu.get_barrier_semaphore()
    for o in range(1, n_mod):
        pl.semaphore_signal(barrier, inc=1, device_id={"mod": mod_at[o]}, device_id_type=MESH)
    for h in range(1, n_hi):
        pl.semaphore_signal(barrier, inc=1, device_id={"dp": hi_at[h]}, device_id_type=MESH)
    if n_lo == 2:
        sibling = hi * 2 + (1 - lo)
        pl.semaphore_signal(barrier, inc=1, device_id={"dp": sibling}, device_id_type=MESH)
    for copy in mine:
        copy.wait()

    token = lax.broadcasted_iota(jnp.int32, (seq, LANES), 0)
    lane = lax.broadcasted_iota(jnp.int32, (ex, LANES), 1)

    def module_tile(j):
        columns = pl.ds(pl.multiple_of(j * LANES, LANES), LANES)
        for e in range(ex):
            grad = grad_v[e, :, columns].astype(jnp.float32)
            grad = jnp.where(token < lens_ref[e], grad, 0.0).astype(jnp.bfloat16)
            prod[pl.ds(e * LANES, LANES), :] = lax.dot_general(
                grad, act_v[e, :, columns], (((0,), (0,)), ((), ())),
                preferred_element_type=jnp.float32)
        for mm in range(per_tile):
            rows = []
            for t in range(tiles):
                row = None
                for k in range(per_tile):
                    part = prod[pl.ds(mm * rank + t * per_tile + k, ex, stride=LANES), :]
                    shift = (k - mm) % per_tile
                    if shift:
                        part = pltpu.roll(part, shift * rank, 1)
                    row = part if k == 0 else jnp.where(lane >= k * rank, part, row)
                rows.append(row)
            top = functools.reduce(jnp.maximum, [jnp.abs(row) for row in rows])
            power = jnp.ceil(jnp.log2(jnp.maximum(top, 1e-30) * (1.0 / 32766.0)))
            scale = jnp.exp2(-power)
            slot = j * per_tile + mm
            for t in range(tiles):
                coded[slot, :, t * LANES:(t + 1) * LANES] = (
                    jnp.round(rows[t] * scale).astype(jnp.int32).astype(jnp.int16))
            coded[slot, :, entries:] = power.astype(jnp.int32).astype(jnp.int16)

    if width == LANES:
        module_tile(0)
    else:
        lax.fori_loop(0, width // LANES, lambda j, c: (module_tile(j), c)[1], 0)

    peers = (n_mod - 1) + (n_hi - 1) + (n_lo - 1)
    pl.semaphore_wait(barrier, peers)

    def source(position):
        found = jnp.int32(0)
        for m in range(n_mod):
            found = jnp.where(assign_ref[m] == position, m, found)
        return found

    def slot_of(dp_index, mod_index):
        return dp_index * n_mod + mod_index

    def remote(src, dst, send, recv, device):
        return pltpu.make_async_remote_copy(
            src_ref=src, dst_ref=dst, send_sem=send, recv_sem=recv,
            device_id=device, device_id_type=MESH)

    started = []
    z_copies = [None] * n_mod
    for o in list(range(1, n_mod)) + [0]:
        block = coded[source(mod_at[o])]
        if o == 0:
            inbox[slot_of(dp, mod)] = block
        else:
            outbox[o] = block
            z_copies[o] = remote(outbox.at[o], inbox.at[slot_of(dp, mod)],
                                 z_send.at[o], z_recv.at[o], {"mod": mod_at[o]})
            z_copies[o].start()
            started.append(z_copies[o])

    def decode(position, block):
        def tile(t):
            columns = pl.ds(pl.multiple_of(t * LANES, LANES), LANES)
            value = inbox[block, :, columns].astype(jnp.int32).astype(jnp.float32)
            power = inbox[block, :, entries:].astype(jnp.int32).astype(jnp.float32)
            value = value * jnp.exp2(power)
            top = value.astype(jnp.bfloat16)
            rows = pl.ds(position * ex, ex)
            high[rows, columns] = top
            low[rows, columns] = (value - top.astype(jnp.float32)).astype(jnp.bfloat16)
        if small:
            for t in range(tiles):
                tile(t)
        else:
            lax.fori_loop(0, tiles, lambda t, c: (tile(t), c)[1], 0)

    out_rows = out_ref.shape[0] // tiles
    depth = n_lo * n_mod * ex
    inverse_count = 1.0 / (ex * n_mod * n_dp)

    def multiply(h):
        deep = pl.ds(h * depth, depth)
        left = pl.ds(pl.multiple_of(dp * out_rows, LANES), out_rows)
        left_high = high[deep, left].T
        left_low = low[deep, left].T

        def column(t):
            columns = pl.ds(pl.multiple_of(t * LANES, LANES), LANES)
            dot = functools.partial(jnp.dot, preferred_element_type=jnp.float32)
            total = (dot(left_high, high[deep, columns]) + dot(left_high, low[deep, columns])
                     + dot(left_low, high[deep, columns]))
            place = pl.ds(t, out_rows, stride=tiles)
            if h > 0:
                total = total + out_ref[place, :]
            if h == n_hi - 1:
                total = total * inverse_count
            out_ref[place, :] = total
        if small:
            for t in range(tiles):
                column(t)
        else:
            lax.fori_loop(0, tiles, lambda t, c: (column(t), c)[1], 0)

    x_copies = [[None] * n_mod for _ in range(n_hi)]
    c_copies = [None] * n_mod
    f_copies = [[None] * n_mod for _ in range(n_hi)]
    for o in range(n_mod):
        if o:
            z_copies[o].wait_recv()
        block = slot_of(dp, mod_from[o])
        for h in range(1, n_hi):
            x_copies[h][o] = remote(inbox.at[block], inbox.at[block],
                                    x_send.at[h, o], x_recv.at[h, o], {"dp": hi_at[h]})
            x_copies[h][o].start()
            started.append(x_copies[h][o])
        if n_lo == 2:
            c_copies[o] = remote(inbox.at[block], inbox.at[block],
                                 c_send.at[o], c_recv.at[o], {"dp": sibling})
            c_copies[o].start()
            started.append(c_copies[o])
        decode(o, block)
    if n_lo == 2:
        for o in range(n_mod):
            for h in range(1, n_hi):
                x_copies[h][o].wait_recv()
                block = slot_of(hi_from[h] * n_lo + lo, mod_from[o])
                f_copies[h][o] = remote(inbox.at[block], inbox.at[block],
                                        f_send.at[h, o], f_recv.at[h, o], {"dp": sibling})
                f_copies[h][o].start()
                started.append(f_copies[h][o])
            c_copies[o].wait_recv()
            decode(n_mod + o, slot_of(sibling, mod_from[o]))
    multiply(0)
    for h in range(1, n_hi):
        for o in range(n_mod):
            if n_lo == 1:
                x_copies[h][o].wait_recv()
            decode(h * n_lo * n_mod + o, slot_of(hi_from[h] * n_lo + lo, mod_from[o]))
        if n_lo == 2:
            for o in range(n_mod):
                f_copies[h][o].wait_recv()
                decode((h * n_lo + 1) * n_mod + o, slot_of(hi_from[h] * 2 + (1 - lo), mod_from[o]))
        multiply(h)
    for copy in started:
        copy.wait_send()


def solution(mesh):
    n_mod, n_dp = mesh.shape["mod"], mesh.shape["dp"]

    def body(act_proj, grad_proj, lengths, assignment):
        ex, seq, width = act_proj.shape
        rank = width // assignment.shape[0]
        entries = rank * rank
        out_rows = entries // n_dp
        tiles = entries // LANES
        n_hi = n_dp // 2 if n_dp % 2 == 0 else n_dp
        dma = pltpu.SemaphoreType.DMA
        in_hbm = pl.BlockSpec(memory_space=pltpu.HBM)
        result = pl.pallas_call(
            functools.partial(kernel, n_mod, n_dp, rank),
            out_shape=jax.ShapeDtypeStruct((out_rows * tiles, LANES), jnp.float32),
            in_specs=[in_hbm] * 4,
            out_specs=pl.BlockSpec(memory_space=pltpu.VMEM),
            scratch_shapes=[
                pltpu.SMEM(lengths.shape, jnp.int32),
                pltpu.SMEM(assignment.shape, jnp.int32),
                pltpu.VMEM(act_proj.shape, jnp.bfloat16),
                pltpu.VMEM(grad_proj.shape, jnp.bfloat16),
                pltpu.VMEM((ex * LANES, LANES), jnp.float32),
                pltpu.VMEM((n_mod, ex, entries + LANES), jnp.int16),
                pltpu.VMEM((n_mod, ex, entries + LANES), jnp.int16),
                pltpu.VMEM((n_dp * n_mod, ex, entries + LANES), jnp.int16),
                pltpu.VMEM((n_dp * n_mod * ex, entries), jnp.bfloat16),
                pltpu.VMEM((n_dp * n_mod * ex, entries), jnp.bfloat16),
                dma((4,)),
                dma((n_mod,)), dma((n_mod,)),
                dma((n_hi, n_mod)), dma((n_hi, n_mod)),
                dma((n_mod,)), dma((n_mod,)),
                dma((n_hi, n_mod)), dma((n_hi, n_mod)),
            ],
            compiler_params=pltpu.CompilerParams(
                collective_id=0, has_side_effects=True, vmem_limit_bytes=48 * 1024 * 1024),
        )(*[pltpu.with_memory_space_constraint(x, pltpu.HBM)
            for x in (lengths, assignment, act_proj, grad_proj)])
        return result.reshape(out_rows, 1, entries)

    return jax.shard_map(
        body,
        mesh=mesh,
        in_specs=(
            P(("grp", "mod", "dp"), None, None),
            P(("grp", "mod", "dp"), None, None),
            P(("grp", "mod", "dp")),
            P(),
        ),
        out_specs=P(("grp", "dp"), "mod", None),
        check_vma=False,
    )
```

```python
import functools

import jax
import jax.numpy as jnp
from jax import lax
from jax.experimental import pallas as pl
from jax.experimental.pallas import tpu as pltpu
from jax.sharding import PartitionSpec as P

MESH = pl.DeviceIdType.MESH
LANES = 128


def kernel(
    n_mod, n_dp, rank, lens_hbm, assign_hbm, act_hbm, grad_hbm, out_ref,
    lens_ref, assign_ref, act_v, grad_v, prod, coded, outbox, inbox, high, low,
    in_sem, z_send, z_recv, x_send, x_recv, c_send, c_recv, f_send, f_recv,
):
    ex, seq, width = act_v.shape
    entries = rank * rank
    tiles = entries // LANES
    per_tile = LANES // rank
    n_lo = 2 if n_dp % 2 == 0 else 1
    n_hi = n_dp // n_lo
    small = n_mod <= 8
    direct = n_mod - 1
    mod = lax.axis_index("mod")
    dp = lax.axis_index("dp")
    hi, lo = dp // n_lo, dp % n_lo
    mine = [pltpu.make_async_copy(act_hbm, act_v, in_sem.at[0]),
            pltpu.make_async_copy(grad_hbm, grad_v, in_sem.at[1]),
            pltpu.make_async_copy(lens_hbm, lens_ref, in_sem.at[2]),
            pltpu.make_async_copy(assign_hbm, assign_ref, in_sem.at[3])]
    for copy in mine:
        copy.start()

    def by_distance(k):
        upper = jnp.where(mod + k < n_mod, mod + k, n_mod - 1 - k)
        lower = jnp.where(k <= mod, mod - k, k)
        return jnp.where(mod >= n_mod // 2, upper, lower)

    near = [mod] + [by_distance(k) for k in range(1, n_mod)]
    hi_at = [lax.rem(hi + h, n_hi) * n_lo + lo for h in range(n_hi)]

    def across(dp_index):
        return dp_index + 1 - 2 * lo

    hi_from = [lax.rem(hi + n_hi - h, n_hi) for h in range(n_hi)]

    barrier = pltpu.get_barrier_semaphore()
    for o in range(1, n_mod):
        pl.semaphore_signal(barrier, inc=1, device_id={"mod": near[o]}, device_id_type=MESH)
    for h in range(1, n_hi):
        pl.semaphore_signal(barrier, inc=1, device_id={"dp": hi_at[h]}, device_id_type=MESH)
        if n_lo == 2 and direct < n_mod:
            pl.semaphore_signal(barrier, inc=1, device_id={"dp": across(hi_at[h])}, device_id_type=MESH)
    if n_lo == 2:
        sibling = hi * 2 + (1 - lo)
        pl.semaphore_signal(barrier, inc=1, device_id={"dp": sibling}, device_id_type=MESH)
    for copy in mine:
        copy.wait()

    token = lax.broadcasted_iota(jnp.int32, (seq, LANES), 0)
    lane = lax.broadcasted_iota(jnp.int32, (ex, LANES), 1)

    def module_tile(j):
        columns = pl.ds(pl.multiple_of(j * LANES, LANES), LANES)
        for e in range(ex):
            grad = grad_v[e, :, columns].astype(jnp.float32)
            grad = jnp.where(token < lens_ref[e], grad, 0.0).astype(jnp.bfloat16)
            prod[pl.ds(e * LANES, LANES), :] = lax.dot_general(
                grad, act_v[e, :, columns], (((0,), (0,)), ((), ())),
                preferred_element_type=jnp.float32)
        for mm in range(per_tile):
            rows = []
            for t in range(tiles):
                row = None
                for k in range(per_tile):
                    part = prod[pl.ds(mm * rank + t * per_tile + k, ex, stride=LANES), :]
                    shift = (k - mm) % per_tile
                    if shift:
                        part = pltpu.roll(part, shift * rank, 1)
                    row = part if k == 0 else jnp.where(lane >= k * rank, part, row)
                rows.append(row)
            top = functools.reduce(jnp.maximum, [jnp.abs(row) for row in rows])
            power = jnp.ceil(jnp.log2(jnp.maximum(top, 1e-30) * (1.0 / 32766.0)))
            scale = jnp.exp2(-power)
            slot = j * per_tile + mm
            for t in range(tiles):
                coded[slot, :, t * LANES:(t + 1) * LANES] = (
                    jnp.round(rows[t] * scale).astype(jnp.int32).astype(jnp.int16))
            coded[slot, :, entries:] = power.astype(jnp.int32).astype(jnp.int16)

    if width == LANES:
        module_tile(0)
    else:
        lax.fori_loop(0, width // LANES, lambda j, c: (module_tile(j), c)[1], 0)

    peers = (n_mod - 1) + (n_hi - 1) * (2 if n_lo == 2 and direct < n_mod else 1) + (n_lo - 1)
    pl.semaphore_wait(barrier, peers)

    def source(position):
        found = jnp.int32(0)
        for m in range(n_mod):
            found = jnp.where(assign_ref[m] == position, m, found)
        return found

    def slot_of(dp_index, mod_index):
        return dp_index * n_mod + mod_index

    def remote(src, dst, send, recv, device):
        return pltpu.make_async_remote_copy(
            src_ref=src, dst_ref=dst, send_sem=send, recv_sem=recv,
            device_id=device, device_id_type=MESH)

    started = []
    z_copies = [None] * n_mod
    for o in range(n_mod - 1, -1, -1):
        block = coded[source(near[o])]
        if o == 0:
            inbox[slot_of(dp, mod)] = block
        else:
            outbox[o] = block
            z_copies[o] = remote(outbox.at[o], inbox.at[slot_of(dp, mod)],
                                 z_send.at[o], z_recv.at[mod], {"mod": near[o]})
            z_copies[o].start()
            started.append(z_copies[o])

    def decode(position, block):
        def tile(t):
            columns = pl.ds(pl.multiple_of(t * LANES, LANES), LANES)
            value = inbox[block, :, columns].astype(jnp.int32).astype(jnp.float32)
            power = inbox[block, :, entries:].astype(jnp.int32).astype(jnp.float32)
            value = value * jnp.exp2(power)
            top = value.astype(jnp.bfloat16)
            rows = pl.ds(position * ex, ex)
            high[rows, columns] = top
            low[rows, columns] = (value - top.astype(jnp.float32)).astype(jnp.bfloat16)
        if small:
            for t in range(tiles):
                tile(t)
        else:
            lax.fori_loop(0, tiles, lambda t, c: (tile(t), c)[1], 0)

    out_rows = out_ref.shape[0] // tiles
    depth = n_lo * n_mod * ex
    inverse_count = 1.0 / (ex * n_mod * n_dp)

    def multiply(h):
        deep = pl.ds(h * depth, depth)
        left = pl.ds(pl.multiple_of(dp * out_rows, LANES), out_rows)
        left_high = high[deep, left].T
        left_low = low[deep, left].T

        def column(t):
            columns = pl.ds(pl.multiple_of(t * LANES, LANES), LANES)
            dot = functools.partial(jnp.dot, preferred_element_type=jnp.float32)
            total = (dot(left_high, high[deep, columns]) + dot(left_high, low[deep, columns])
                     + dot(left_low, high[deep, columns]))
            place = pl.ds(t, out_rows, stride=tiles)
            if h > 0:
                total = total + out_ref[place, :]
            if h == n_hi - 1:
                total = total * inverse_count
            out_ref[place, :] = total
        if small:
            for t in range(tiles):
                column(t)
        else:
            lax.fori_loop(0, tiles, lambda t, c: (column(t), c)[1], 0)

    x_copies = [[None] * n_mod for _ in range(n_hi)]
    c_copies = [None] * n_mod
    f_copies = [[None] * n_mod for _ in range(n_hi)]
    for o in range(n_mod):
        block = slot_of(dp, near[o])
        if o:
            remote(inbox.at[block], inbox.at[block], z_send.at[o], z_recv.at[near[o]],
                   {"mod": near[o]}).wait_recv()
        for h in range(1, n_hi):
            x_copies[h][o] = remote(inbox.at[block], inbox.at[block],
                                    x_send.at[h, o], x_recv.at[h, o], {"dp": hi_at[h]})
            x_copies[h][o].start()
            started.append(x_copies[h][o])
            if n_lo == 2 and o >= direct:
                f_copies[h][o] = remote(inbox.at[block], inbox.at[block],
                                        f_send.at[h, o], f_recv.at[h, o], {"dp": across(hi_at[h])})
                f_copies[h][o].start()
                started.append(f_copies[h][o])
        if n_lo == 2:
            c_copies[o] = remote(inbox.at[block], inbox.at[block],
                                 c_send.at[o], c_recv.at[o], {"dp": sibling})
            c_copies[o].start()
            started.append(c_copies[o])
        decode(o, block)
    if n_lo == 2:
        for o in range(n_mod):
            for h in range(1, n_hi):
                if o < direct:
                    x_copies[h][o].wait_recv()
                    block = slot_of(hi_from[h] * n_lo + lo, near[o])
                    f_copies[h][o] = remote(inbox.at[block], inbox.at[block],
                                            f_send.at[h, o], f_recv.at[h, o], {"dp": sibling})
                    f_copies[h][o].start()
                    started.append(f_copies[h][o])
            c_copies[o].wait_recv()
            decode(n_mod + o, slot_of(sibling, near[o]))
    multiply(0)
    for h in range(1, n_hi):
        for o in range(n_mod):
            if n_lo == 1 or o >= direct:
                x_copies[h][o].wait_recv()
            decode(h * n_lo * n_mod + o, slot_of(hi_from[h] * n_lo + lo, near[o]))
            if n_lo == 2:
                block = slot_of(hi_from[h] * 2 + (1 - lo), near[o])
                remote(inbox.at[block], inbox.at[block], f_send.at[h, o], f_recv.at[h, o],
                       {"dp": sibling}).wait_recv()
                decode((h * n_lo + 1) * n_mod + o, block)
        multiply(h)
    for copy in started:
        copy.wait_send()


def solution(mesh):
    n_mod, n_dp = mesh.shape["mod"], mesh.shape["dp"]

    def body(act_proj, grad_proj, lengths, assignment):
        ex, seq, width = act_proj.shape
        rank = width // assignment.shape[0]
        entries = rank * rank
        out_rows = entries // n_dp
        tiles = entries // LANES
        n_hi = n_dp // 2 if n_dp % 2 == 0 else n_dp
        dma = pltpu.SemaphoreType.DMA
        in_hbm = pl.BlockSpec(memory_space=pltpu.HBM)
        result = pl.pallas_call(
            functools.partial(kernel, n_mod, n_dp, rank),
            out_shape=jax.ShapeDtypeStruct((out_rows * tiles, LANES), jnp.float32),
            in_specs=[in_hbm] * 4,
            out_specs=pl.BlockSpec(memory_space=pltpu.VMEM),
            scratch_shapes=[
                pltpu.SMEM(lengths.shape, jnp.int32),
                pltpu.SMEM(assignment.shape, jnp.int32),
                pltpu.VMEM(act_proj.shape, jnp.bfloat16),
                pltpu.VMEM(grad_proj.shape, jnp.bfloat16),
                pltpu.VMEM((ex * LANES, LANES), jnp.float32),
                pltpu.VMEM((n_mod, ex, entries + LANES), jnp.int16),
                pltpu.VMEM((n_mod, ex, entries + LANES), jnp.int16),
                pltpu.VMEM((n_dp * n_mod, ex, entries + LANES), jnp.int16),
                pltpu.VMEM((n_dp * n_mod * ex, entries), jnp.bfloat16),
                pltpu.VMEM((n_dp * n_mod * ex, entries), jnp.bfloat16),
                dma((4,)),
                dma((n_mod,)), dma((n_mod,)),
                dma((n_hi, n_mod)), dma((n_hi, n_mod)),
                dma((n_mod,)), dma((n_mod,)),
                dma((n_hi, n_mod)), dma((n_hi, n_mod)),
            ],
            compiler_params=pltpu.CompilerParams(
                collective_id=0, has_side_effects=True, vmem_limit_bytes=48 * 1024 * 1024),
        )(*[pltpu.with_memory_space_constraint(x, pltpu.HBM)
            for x in (lengths, assignment, act_proj, grad_proj)])
        return result.reshape(out_rows, 1, entries)

    return jax.shard_map(
        body,
        mesh=mesh,
        in_specs=(
            P(("grp", "mod", "dp"), None, None),
            P(("grp", "mod", "dp"), None, None),
            P(("grp", "mod", "dp")),
            P(),
        ),
        out_specs=P(("grp", "dp"), "mod", None),
        check_vma=False,
    )
```

```python
import functools

import jax
import jax.numpy as jnp
from jax import lax
from jax.experimental import pallas as pl
from jax.experimental.pallas import tpu as pltpu
from jax.sharding import PartitionSpec as P

MESH = pl.DeviceIdType.MESH
LANES = 128


def kernel(
    n_mod, n_dp, rank, lens_hbm, assign_hbm, act_hbm, grad_hbm, out_ref,
    lens_ref, assign_ref, act_v, grad_v, prod, coded, outbox, inbox, high, low,
    in_sem, z_send, z_recv, x_send, x_recv, c_send, c_recv, f_send, f_recv,
):
    ex, seq, width = act_v.shape
    entries = rank * rank
    tiles = entries // LANES
    per_tile = LANES // rank
    n_lo = 2 if n_dp % 2 == 0 else 1
    n_hi = n_dp // n_lo
    small = n_mod <= 8
    direct = n_mod - 1
    mod = lax.axis_index("mod")
    dp = lax.axis_index("dp")
    hi, lo = dp // n_lo, dp % n_lo
    mine = [pltpu.make_async_copy(act_hbm, act_v, in_sem.at[0]),
            pltpu.make_async_copy(grad_hbm, grad_v, in_sem.at[1]),
            pltpu.make_async_copy(lens_hbm, lens_ref, in_sem.at[2]),
            pltpu.make_async_copy(assign_hbm, assign_ref, in_sem.at[3])]
    for copy in mine:
        copy.start()

    def by_distance(k):
        upper = jnp.where(mod + k < n_mod, mod + k, n_mod - 1 - k)
        lower = jnp.where(k <= mod, mod - k, k)
        return jnp.where(mod >= n_mod // 2, upper, lower)

    near = [mod] + [by_distance(k) for k in range(1, n_mod)]
    hi_at = [lax.rem(hi + h, n_hi) * n_lo + lo for h in range(n_hi)]

    def across(dp_index):
        return dp_index + 1 - 2 * lo

    hi_from = [lax.rem(hi + n_hi - h, n_hi) for h in range(n_hi)]

    barrier = pltpu.get_barrier_semaphore()
    for o in range(1, n_mod):
        pl.semaphore_signal(barrier, inc=1, device_id={"mod": near[o]}, device_id_type=MESH)
    for h in range(1, n_hi):
        pl.semaphore_signal(barrier, inc=1, device_id={"dp": hi_at[h]}, device_id_type=MESH)
        if n_lo == 2 and direct < n_mod:
            pl.semaphore_signal(barrier, inc=1, device_id={"dp": across(hi_at[h])}, device_id_type=MESH)
    if n_lo == 2:
        sibling = hi * 2 + (1 - lo)
        pl.semaphore_signal(barrier, inc=1, device_id={"dp": sibling}, device_id_type=MESH)
    for copy in mine:
        copy.wait()

    token = lax.broadcasted_iota(jnp.int32, (seq, LANES), 0)
    lane = lax.broadcasted_iota(jnp.int32, (ex, LANES), 1)

    def module_tile(j):
        columns = pl.ds(pl.multiple_of(j * LANES, LANES), LANES)
        for e in range(ex):
            grad = grad_v[e, :, columns].astype(jnp.float32)
            grad = jnp.where(token < lens_ref[e], grad, 0.0).astype(jnp.bfloat16)
            prod[pl.ds(e * LANES, LANES), :] = lax.dot_general(
                grad, act_v[e, :, columns], (((0,), (0,)), ((), ())),
                preferred_element_type=jnp.float32)
        for mm in range(per_tile):
            rows = []
            for t in range(tiles):
                row = None
                for k in range(per_tile):
                    part = prod[pl.ds(mm * rank + t * per_tile + k, ex, stride=LANES), :]
                    shift = (k - mm) % per_tile
                    if shift:
                        part = pltpu.roll(part, shift * rank, 1)
                    row = part if k == 0 else jnp.where(lane >= k * rank, part, row)
                rows.append(row)
            top = functools.reduce(jnp.maximum, [jnp.abs(row) for row in rows])
            power = jnp.ceil(jnp.log2(jnp.maximum(top, 1e-30) * (1.0 / 32766.0)))
            scale = jnp.exp2(-power)
            slot = j * per_tile + mm
            for t in range(tiles):
                coded[slot, :, t * LANES:(t + 1) * LANES] = (
                    jnp.round(rows[t] * scale).astype(jnp.int32).astype(jnp.int16))
            coded[slot, :, entries:] = power.astype(jnp.int32).astype(jnp.int16)

    if width == LANES:
        module_tile(0)
    else:
        lax.fori_loop(0, width // LANES, lambda j, c: (module_tile(j), c)[1], 0)

    peers = (n_mod - 1) + (n_hi - 1) * (2 if n_lo == 2 and direct < n_mod else 1) + (n_lo - 1)
    pl.semaphore_wait(barrier, peers)

    def source(position):
        found = jnp.int32(0)
        for m in range(n_mod):
            found = jnp.where(assign_ref[m] == position, m, found)
        return found

    def slot_of(dp_index, mod_index):
        return dp_index * n_mod + mod_index

    def remote(src, dst, send, recv, device):
        return pltpu.make_async_remote_copy(
            src_ref=src, dst_ref=dst, send_sem=send, recv_sem=recv,
            device_id=device, device_id_type=MESH)

    started = []
    z_copies = [None] * n_mod
    for o in range(n_mod - 1, -1, -1):
        block = coded[source(near[o])]
        if o == 0:
            inbox[slot_of(dp, mod)] = block
        else:
            outbox[o] = block
            z_copies[o] = remote(outbox.at[o], inbox.at[slot_of(dp, mod)],
                                 z_send.at[o], z_recv.at[mod], {"mod": near[o]})
            z_copies[o].start()
            started.append(z_copies[o])

    def decode(position, block):
        def tile(t):
            columns = pl.ds(pl.multiple_of(t * LANES, LANES), LANES)
            value = inbox[block, :, columns].astype(jnp.int32).astype(jnp.float32)
            power = inbox[block, :, entries:].astype(jnp.int32).astype(jnp.float32)
            value = value * jnp.exp2(power)
            top = value.astype(jnp.bfloat16)
            rows = pl.ds(position * ex, ex)
            high[rows, columns] = top
            low[rows, columns] = (value - top.astype(jnp.float32)).astype(jnp.bfloat16)
        if small:
            for t in range(tiles):
                tile(t)
        else:
            lax.fori_loop(0, tiles, lambda t, c: (tile(t), c)[1], 0)

    out_rows = out_ref.shape[0] // tiles
    depth = n_lo * n_mod * ex
    inverse_count = 1.0 / (ex * n_mod * n_dp)

    def multiply(h):
        deep = pl.ds(h * depth, depth)
        left = pl.ds(pl.multiple_of(dp * out_rows, LANES), out_rows)
        left_high = high[deep, left].T
        left_low = low[deep, left].T
        left_all = jnp.concatenate([left_high, left_high, left_low], axis=1)

        def column(t):
            columns = pl.ds(pl.multiple_of(t * LANES, LANES), LANES)
            right_high = high[deep, columns]
            right_all = jnp.concatenate([right_high, low[deep, columns], right_high], axis=0)
            total = jnp.dot(left_all, right_all, preferred_element_type=jnp.float32)
            place = pl.ds(t, out_rows, stride=tiles)
            if h > 0:
                total = total + out_ref[place, :]
            if h == n_hi - 1:
                total = total * inverse_count
            out_ref[place, :] = total
        if small:
            for t in range(tiles):
                column(t)
        else:
            lax.fori_loop(0, tiles, lambda t, c: (column(t), c)[1], 0)

    x_copies = [[None] * n_mod for _ in range(n_hi)]
    c_copies = [None] * n_mod
    f_copies = [[None] * n_mod for _ in range(n_hi)]
    for o in range(n_mod):
        block = slot_of(dp, near[o])
        if o:
            remote(inbox.at[block], inbox.at[block], z_send.at[o], z_recv.at[near[o]],
                   {"mod": near[o]}).wait_recv()
        for h in range(1, n_hi):
            x_copies[h][o] = remote(inbox.at[block], inbox.at[block],
                                    x_send.at[h, o], x_recv.at[h, o], {"dp": hi_at[h]})
            x_copies[h][o].start()
            started.append(x_copies[h][o])
            if n_lo == 2 and o >= direct:
                f_copies[h][o] = remote(inbox.at[block], inbox.at[block],
                                        f_send.at[h, o], f_recv.at[h, o], {"dp": across(hi_at[h])})
                f_copies[h][o].start()
                started.append(f_copies[h][o])
        if n_lo == 2:
            c_copies[o] = remote(inbox.at[block], inbox.at[block],
                                 c_send.at[o], c_recv.at[o], {"dp": sibling})
            c_copies[o].start()
            started.append(c_copies[o])
        decode(o, block)
    if n_lo == 2:
        for o in range(n_mod):
            for h in range(1, n_hi):
                if o < direct:
                    x_copies[h][o].wait_recv()
                    block = slot_of(hi_from[h] * n_lo + lo, near[o])
                    f_copies[h][o] = remote(inbox.at[block], inbox.at[block],
                                            f_send.at[h, o], f_recv.at[h, o], {"dp": sibling})
                    f_copies[h][o].start()
                    started.append(f_copies[h][o])
            c_copies[o].wait_recv()
            decode(n_mod + o, slot_of(sibling, near[o]))
    multiply(0)
    for h in range(1, n_hi):
        for o in range(n_mod):
            if n_lo == 1 or o >= direct:
                x_copies[h][o].wait_recv()
            decode(h * n_lo * n_mod + o, slot_of(hi_from[h] * n_lo + lo, near[o]))
            if n_lo == 2:
                block = slot_of(hi_from[h] * 2 + (1 - lo), near[o])
                remote(inbox.at[block], inbox.at[block], f_send.at[h, o], f_recv.at[h, o],
                       {"dp": sibling}).wait_recv()
                decode((h * n_lo + 1) * n_mod + o, block)
        multiply(h)
    for copy in started:
        copy.wait_send()


def solution(mesh):
    n_mod, n_dp = mesh.shape["mod"], mesh.shape["dp"]

    def body(act_proj, grad_proj, lengths, assignment):
        ex, seq, width = act_proj.shape
        rank = width // assignment.shape[0]
        entries = rank * rank
        out_rows = entries // n_dp
        tiles = entries // LANES
        n_hi = n_dp // 2 if n_dp % 2 == 0 else n_dp
        dma = pltpu.SemaphoreType.DMA
        in_hbm = pl.BlockSpec(memory_space=pltpu.HBM)
        result = pl.pallas_call(
            functools.partial(kernel, n_mod, n_dp, rank),
            out_shape=jax.ShapeDtypeStruct((out_rows * tiles, LANES), jnp.float32),
            in_specs=[in_hbm] * 4,
            out_specs=pl.BlockSpec(memory_space=pltpu.VMEM),
            scratch_shapes=[
                pltpu.SMEM(lengths.shape, jnp.int32),
                pltpu.SMEM(assignment.shape, jnp.int32),
                pltpu.VMEM(act_proj.shape, jnp.bfloat16),
                pltpu.VMEM(grad_proj.shape, jnp.bfloat16),
                pltpu.VMEM((ex * LANES, LANES), jnp.float32),
                pltpu.VMEM((n_mod, ex, entries + LANES), jnp.int16),
                pltpu.VMEM((n_mod, ex, entries + LANES), jnp.int16),
                pltpu.VMEM((n_dp * n_mod, ex, entries + LANES), jnp.int16),
                pltpu.VMEM((n_dp * n_mod * ex, entries), jnp.bfloat16),
                pltpu.VMEM((n_dp * n_mod * ex, entries), jnp.bfloat16),
                dma((4,)),
                dma((n_mod,)), dma((n_mod,)),
                dma((n_hi, n_mod)), dma((n_hi, n_mod)),
                dma((n_mod,)), dma((n_mod,)),
                dma((n_hi, n_mod)), dma((n_hi, n_mod)),
            ],
            compiler_params=pltpu.CompilerParams(
                collective_id=0, has_side_effects=True, vmem_limit_bytes=48 * 1024 * 1024),
        )(*[pltpu.with_memory_space_constraint(x, pltpu.HBM)
            for x in (lengths, assignment, act_proj, grad_proj)])
        return result.reshape(out_rows, 1, entries)

    return jax.shard_map(
        body,
        mesh=mesh,
        in_specs=(
            P(("grp", "mod", "dp"), None, None),
            P(("grp", "mod", "dp"), None, None),
            P(("grp", "mod", "dp")),
            P(),
        ),
        out_specs=P(("grp", "dp"), "mod", None),
        check_vma=False,
    )
```
